32 devices in a mesh: grp: 2 (over x), dev: 4 (over y, core), role: 4 (over z).
Axes of the slice: x: 2, y: 2, z: 4, core: 2. Of those that a mesh axis runs over, the one named last changes fastest.
Arguments:
- queries: bfloat16 [256, 4096], P(('grp', 'dev', 'role')), parts along dimension 0, may hold values from -16 to 16
- key_cache: bfloat16 [256, 128, 512], P(('grp', 'dev', 'role')), parts along dimension 0, may hold values from -8 to 8
- value_cache: bfloat16 [256, 128, 512], P(('grp', 'dev', 'role')), parts along dimension 0, may hold values from -6 to 6
- new_key: bfloat16 [256, 512], P(('grp', 'dev', 'role')), parts along dimension 0, may hold values from -8 to 8
- new_value: bfloat16 [256, 512], P(('grp', 'dev', 'role')), parts along dimension 0, may hold values from -6 to 6
- lengths: int32 [256], P(('grp', 'dev', 'role')), parts along dimension 0, may hold values from 1 to 128, as said below
- residual: bfloat16 [256, 4096], P(('grp', 'dev', 'role')), parts along dimension 0, may hold values from -40 to 40
- out_proj: bfloat16 [4096, 4096], P(None, ('dev', 'role')), may hold values from -0.09375 to 0.09375
- norm_gain: float32 [4096], replicated, may hold values from 0.25 to 1.75
- expert_ids: int32 [256, 8], P(('grp', 'dev', 'role')), parts along dimension 0, may hold values from 0 to 63, all different within a row; in each aligned block of 8 rows (0 to 7, 8 to 15, ...) at most 2 rows name the same one
- gate_weights: float32 [256, 8], P(('grp', 'dev', 'role')), parts along dimension 0, may hold values from 0.03 to 0.6
- w_gate: bfloat16 [128, 4096, 384], P(('dev', 'role')), may hold values from -0.09375 to 0.09375
- w_up: bfloat16 [128, 4096, 384], P(('dev', 'role')), may hold values from -0.09375 to 0.09375
- w_down: bfloat16 [128, 384, 4096], P(('dev', 'role')), may hold values from -0.21875 to 0.21875
Outputs:
- mixed: bfloat16 [256, 4096], P(('grp', 'dev', 'role')), parts along dimension 0
The draws below stay inside these ranges and needn't reach their ends.
There are 2 independent parts, one for each index of `grp`. The reference program is written for one: setup_inputs(seed, part) draws one part's arguments, and reference() takes and returns one part's arrays. A program takes and returns all parts, laid end to end along the dimension named above; an argument that names none is the same for every part. Nothing has to cross between parts.
Inputs may be any that keep to these rules, and one draw needn't show every extreme that they name: `expert_ids`: each row names 8 different experts; among the rows of one device no expert is named more than 2 times, a bound that some block reaches. `lengths`: the first row of each part holds 128 positions.
All inputs are finite; a program needn't handle non-finite values.
Results may differ from the reference program's by a relative error of at most 0.0053.
Values may be sent and summed in bfloat16 or wider, within the bound.
A program may use at most 192 MiB of HBM per device.

```python
import math
import jax
import jax.numpy as jnp
import numpy as np
from jax import lax

D = 4096
QH = 32
KV = 4
HD = 128
EXPERTS = 64
HALF = 384
TOP = 8
ROWS = 8
CTX = 128
CAP = 2
TOKENS = 128
N_DEV = 4
N_ROLE = 4


def draw_queries(key, part):
    key = jax.random.fold_in(key, 11)
    base = jnp.clip(jax.random.normal(key, (TOKENS, KV, QH // KV, HD), jnp.float32), -6.0, 6.0)
    return base.reshape(TOKENS, QH * HD).astype(jnp.bfloat16)


def draw_key_cache(key, part):
    key = jax.random.fold_in(key, 12)
    base = jnp.clip(jax.random.normal(key, (TOKENS, CTX, KV, HD), jnp.float32), -6.0, 6.0)
    return base.reshape(TOKENS, CTX, KV * HD).astype(jnp.bfloat16)


def draw_new_key(key, part):
    key = jax.random.fold_in(key, 13)
    base = jnp.clip(jax.random.normal(key, (TOKENS, KV, HD), jnp.float32), -6.0, 6.0)
    return base.reshape(TOKENS, KV * HD).astype(jnp.bfloat16)


def draw_lengths(key, part):
    key = jax.random.fold_in(key, 14)
    drawn = jax.random.randint(key, (TOKENS,), 1, CTX + 1, dtype=jnp.int32)
    return jnp.where(jnp.arange(TOKENS) == 0, CTX, drawn).astype(jnp.int32)


def draw_residual(key, part):
    key = jax.random.fold_in(key, 15)
    first, second, third = jax.random.split(key, 3)
    low = math.log(0.3)
    high = math.log(3.0)
    row_scale = jnp.exp(jax.random.uniform(first, (TOKENS, 1), jnp.float32, low, high))
    column_scale = jnp.exp(jax.random.uniform(second, (1, D), jnp.float32, low, high))
    base = jnp.clip(jax.random.normal(third, (TOKENS, D), jnp.float32), -4.0, 4.0)
    return (base * row_scale * column_scale).astype(jnp.bfloat16)


def block_scale(stream_key, extent, cuts, low, top_value):
    def one(axis_at, shards_of):
        heights = jax.random.uniform(jax.random.fold_in(jax.random.fold_in(stream_key, 6), axis_at), (shards_of,), jnp.float32, low / len(cuts), top_value / len(cuts))
        return jnp.repeat(jnp.exp(heights), extent[axis_at] // shards_of).reshape((-1,) + (1,) * (len(extent) - axis_at - 1))

    level = one(*cuts[0])
    for cut in cuts[1:]:
        level = level * one(*cut)
    return level


def assign_block(own_key, own, number, rows, amount, top, limit, lean):
    ranking = jax.random.permutation(own_key, amount)
    crowded, usual = portions_of(amount, rows * top, limit, lean, True), portions_of(amount, rows * top, limit, lean, False)
    places = jnp.arange(amount)

    def named(tallies, rotation):
        used = int((tallies > 0).sum())
        fixed = max(1, used // 4)
        passed = fixed + (places - fixed + rotation * (used - fixed)) % max(1, amount - fixed)
        return jnp.zeros((amount,), jnp.int32).at[ranking[jnp.where(places < fixed, places, passed)]].set(jnp.asarray(tallies, jnp.int32))

    tallies = jnp.where(number % 4 == 0, named(crowded, number // 4), named(usual, number - number // 4 - 1))
    mixed = jax.random.permutation(jax.random.fold_in(own, 3), amount)
    source_of, receiver = mixed[0:amount // 2 * 2:2], mixed[1:amount // 2 * 2:2]
    margin = jnp.minimum(tallies[source_of] - 1, limit - tallies[receiver]) // 2
    margin = jnp.where((source_of == ranking[0]) | (receiver == ranking[0]) | (tallies[receiver] == 0), 0, jnp.maximum(margin, 0))
    passed = jax.random.randint(jax.random.fold_in(own, 4), (amount // 2,), 0, 1 << 20) % (margin + 1)
    tallies = tallies.at[source_of].add(-passed).at[receiver].add(passed)
    members = jnp.searchsorted(jnp.cumsum(tallies), jnp.arange(rows * top), side="right").astype(jnp.int32)
    grid = members.reshape(top, rows).T
    grid = grid[jax.random.permutation(jax.random.fold_in(own, 1), rows)]
    rotation = jax.random.randint(jax.random.fold_in(own, 2), (rows, 1), 0, top)
    return jnp.take_along_axis(grid, (jnp.arange(top)[None, :] + rotation) % top, axis=1)


def portions_of(amount, total, bound, slope, full):
    portions = [(1 << 20) // math.isqrt(rank ** slope) + 1 for rank in range(1, amount + 1)]
    largest = bound if full else min(bound, max(-(-total // amount), total * portions[0] // sum(portions)))
    least = 1 if total - largest >= amount - 1 else 0
    given, spare = [largest] + [least] * (amount - 1), total - largest - least * (amount - 1)
    while spare > 0:
        movable = [i for i in range(1, amount) if given[i] < largest] or [i for i in range(1, amount) if given[i] < bound]
        pool, left = sum([portions[i] for i in movable]), spare
        for i in movable:
            addition = min(bound - given[i], max(1, left * portions[i] // pool), spare)
            given[i] = given[i] + addition
            spare = spare - addition
    return np.array(given)


def bell_draw(rng, shape, width, most, cuts=(), kind=jnp.bfloat16):
    array = width * jax.random.normal(rng, shape, jnp.float32)
    if cuts:
        array = array * block_scale(rng, shape, cuts, -0.22, 0.18)
    return jnp.clip(array, -most, most).astype(kind)


def setup_inputs(seed: int = 0, part: int = 0) -> dict:
    splits = jax.random.split(jax.random.key(seed), 15)
    part_splits = jax.random.split(jax.random.fold_in(splits[14], part), 15)
    queries = draw_queries(jax.random.fold_in(jax.random.fold_in(splits[14], part), 71), part)
    key_cache = draw_key_cache(jax.random.fold_in(jax.random.fold_in(splits[14], part), 71), part)
    value_cache = bell_draw(part_splits[2], (TOKENS, CTX, KV * HD), 1.0, 6.0, ((0, 16),))
    new_key = draw_new_key(jax.random.fold_in(jax.random.fold_in(splits[14], part), 71), part)
    new_value = bell_draw(part_splits[4], (TOKENS, KV * HD), 1.0, 6.0, ((0, 16),))
    lengths = draw_lengths(jax.random.fold_in(jax.random.fold_in(splits[14], part), 71), part)
    residual = draw_residual(jax.random.fold_in(jax.random.fold_in(splits[14], part), 71), part)
    out_proj = bell_draw(splits[7], (QH * HD, D), (QH * HD) ** -0.5, 0.09375, ((1, 16),))
    norm_gain = jnp.clip(1.0 + 0.15 * jax.random.normal(splits[8], (D,), jnp.float32), 0.25, 1.75)
    expert_ids_keys = jax.random.split(jax.random.fold_in(part_splits[9], 1), TOKENS // ROWS)
    expert_ids_turns = jax.random.permutation(jax.random.fold_in(part_splits[9], 3), TOKENS // ROWS)
    expert_ids = jax.vmap(lambda own, number: assign_block(jax.random.fold_in(part_splits[9], 2), own, number, ROWS, EXPERTS, TOP, CAP, 2))(expert_ids_keys, expert_ids_turns).reshape((TOKENS, TOP))
    gate_weights = jnp.clip(jnp.exp(math.log(0.6) - 2.9957323 * jax.random.uniform(part_splits[10], (TOKENS, TOP), jnp.float32) ** block_scale(part_splits[10], (TOKENS, TOP), ((0, 16),), -0.2, 0.2)), 0.03, 0.6)
    w_gate = bell_draw(splits[11], (2 * EXPERTS, D, HALF), D ** -0.5, 0.09375, ((0, 16),))
    w_up = bell_draw(splits[12], (2 * EXPERTS, D, HALF), D ** -0.5, 0.09375, ((0, 16),))
    w_down = bell_draw(splits[13], (2 * EXPERTS, HALF, D), (2 * HALF) ** -0.5, 0.21875, ((0, 16),))
    return dict(queries=queries, key_cache=key_cache, value_cache=value_cache, new_key=new_key, new_value=new_value, lengths=lengths, residual=residual, out_proj=out_proj, norm_gain=norm_gain, expert_ids=expert_ids, gate_weights=gate_weights, w_gate=w_gate, w_up=w_up, w_down=w_down)


def attend(pieces):
    queries, keys, values, new_key, new_value, lengths = pieces
    count = queries.shape[0]
    grouped = queries.astype(jnp.float32).reshape(count, KV, QH // KV, HD)
    cached_keys = keys.astype(jnp.float32).reshape(count, CTX, KV, HD)
    cached_values = values.astype(jnp.float32).reshape(count, CTX, KV, HD)
    fresh_key = new_key.astype(jnp.float32).reshape(count, KV, HD)
    fresh_value = new_value.astype(jnp.float32).reshape(count, KV, HD)
    scaling = HD ** (-0.5)
    scores = jnp.einsum('rkgd,rtkd->rkgt', grouped, cached_keys) * scaling
    own_score = jnp.einsum('rkgd,rkd->rkg', grouped, fresh_key) * scaling
    visible = jnp.arange(CTX, dtype=jnp.int32)[None, :] < lengths[:, None]
    scores = jnp.where(visible[:, None, None, :], scores, -jnp.inf)
    highest = jnp.maximum(lax.optimization_barrier(jnp.max(scores, axis=-1)), own_score)
    weights = jnp.exp(scores - highest[..., None])
    own_weight = jnp.exp(own_score - highest)
    total = lax.optimization_barrier(jnp.sum(weights, axis=-1)) + own_weight
    probs = (weights / total[..., None]).astype(jnp.bfloat16)
    own_prob = (own_weight / total).astype(jnp.bfloat16)
    combined = jnp.einsum('rkgt,rtkd->rkgd', probs.astype(jnp.float32), cached_values)
    combined = combined + own_prob.astype(jnp.float32)[..., None] * fresh_value[:, :, None, :]
    return combined.reshape(count, QH * HD).astype(jnp.bfloat16)

def reference(queries, key_cache, value_cache, new_key, new_value, lengths, residual, out_proj, norm_gain, expert_ids, gate_weights, w_gate, w_up, w_down):
    blocks = TOKENS // ROWS
    pieces = (queries.reshape(blocks, ROWS, QH * HD), key_cache.reshape(blocks, ROWS, CTX, KV * HD), value_cache.reshape(blocks, ROWS, CTX, KV * HD), new_key.reshape(blocks, ROWS, KV * HD), new_value.reshape(blocks, ROWS, KV * HD), lengths.reshape(blocks, ROWS))
    attended = lax.map(attend, pieces).reshape(TOKENS, QH * HD)
    projected = jnp.dot(attended, out_proj, preferred_element_type=jnp.float32)
    hidden_state = (residual.astype(jnp.float32) + projected).astype(jnp.bfloat16)
    widened = hidden_state.astype(jnp.float32)
    normed = (widened * lax.rsqrt(lax.optimization_barrier(jnp.mean(widened * widened, axis=-1, keepdims=True)) + 1e-06) * norm_gain).astype(jnp.bfloat16)
    most_rows = CAP * N_DEV * N_ROLE
    gate_pairs = w_gate.reshape(EXPERTS, 2, D, HALF)
    up_pairs = w_up.reshape(EXPERTS, 2, D, HALF)
    down_pairs = w_down.reshape(EXPERTS, 2, HALF, D)

    def one_expert(carry, inputs):
        gate_half, up_half, down_half, expert = inputs
        named = expert_ids == expert
        row_weight = lax.optimization_barrier(jnp.sum(jnp.where(named, gate_weights, jnp.zeros_like(gate_weights)), axis=-1))
        chosen = jnp.any(named, axis=-1)
        picked = jnp.argsort(jnp.where(chosen, 0, 1).astype(jnp.int32), stable=True)[:most_rows].astype(jnp.int32)
        rows_in = normed[picked]
        output = jnp.zeros((most_rows, D), jnp.float32)
        for half in range(2):
            gate_value = jnp.dot(rows_in, gate_half[half], preferred_element_type=jnp.float32)
            up_value = jnp.dot(rows_in, up_half[half], preferred_element_type=jnp.float32)
            activation = (jax.nn.silu(gate_value) * up_value).astype(jnp.bfloat16)
            output = output + jnp.dot(activation, down_half[half], preferred_element_type=jnp.float32)
        carry = carry.at[picked].add(row_weight[picked][:, None] * output)
        return (carry, None)
    start = jnp.zeros((TOKENS, D), jnp.float32)
    routed, _ = lax.scan(one_expert, start, (gate_pairs, up_pairs, down_pairs, jnp.arange(EXPERTS, dtype=jnp.int32)))
    return (widened + routed).astype(jnp.bfloat16)
```

```python
import functools

import jax
import jax.numpy as jnp
from jax import lax
from jax.experimental import pallas as pl
from jax.experimental.pallas import tpu as pltpu
from jax.sharding import PartitionSpec as P

QH = 32
KV = 4
HD = 128
EXPERTS = 64
TOP = 8
CTX = 128


def attend_rows(queries, key_cache, value_cache, new_key, new_value, lengths):
    count = queries.shape[0]
    grouped = queries.reshape(count, KV, QH // KV, HD)
    cached_keys = key_cache.reshape(count, CTX, KV, HD)
    cached_values = value_cache.reshape(count, CTX, KV, HD)
    fresh_key = new_key.reshape(count, KV, HD)
    fresh_value = new_value.reshape(count, KV, HD).astype(jnp.float32)
    scaling = HD ** (-0.5)
    scores = (
        jnp.einsum("rkgd,rtkd->rkgt", grouped, cached_keys, preferred_element_type=jnp.float32)
        * scaling
    )
    own_score = (
        jnp.einsum("rkgd,rkd->rkg", grouped, fresh_key, preferred_element_type=jnp.float32)
        * scaling
    )
    visible = jnp.arange(CTX, dtype=jnp.int32)[None, :] < lengths[:, None]
    scores = jnp.where(visible[:, None, None, :], scores, -jnp.inf)
    highest = jnp.maximum(jnp.max(scores, axis=-1), own_score)
    weights = jnp.exp(scores - highest[..., None])
    own_weight = jnp.exp(own_score - highest)
    total = jnp.sum(weights, axis=-1) + own_weight
    probs = (weights / total[..., None]).astype(jnp.bfloat16)
    own_prob = (own_weight / total).astype(jnp.bfloat16)
    combined = jnp.einsum(
        "rkgt,rtkd->rkgd", probs, cached_values, preferred_element_type=jnp.float32
    )
    combined = combined + own_prob.astype(jnp.float32)[..., None] * fresh_value[:, :, None, :]
    return combined.reshape(count, QH * HD).astype(jnp.bfloat16)


def expert_work(inputs, w_gate, w_up, w_down):
    gate_value = jnp.einsum("pscd,sdh->psch", inputs, w_gate, preferred_element_type=jnp.float32)
    up_value = jnp.einsum("pscd,sdh->psch", inputs, w_up, preferred_element_type=jnp.float32)
    activation = (jax.nn.silu(gate_value) * up_value).astype(jnp.bfloat16)
    return jnp.einsum("psch,shd->pscd", activation, w_down, preferred_element_type=jnp.float32)


def body(
    queries,
    key_cache,
    value_cache,
    new_key,
    new_value,
    lengths,
    residual,
    out_proj,
    norm_gain,
    expert_ids,
    gate_weights,
    w_gate,
    w_up,
    w_down,
):
    count = queries.shape[0]
    capacity = count // 4
    width = residual.shape[1]
    attended = attend_rows(queries, key_cache, value_cache, new_key, new_value, lengths)
    columns = jnp.dot(
        lax.all_gather(attended, ("dev", "role"), axis=0, tiled=True),
        out_proj,
        preferred_element_type=jnp.float32,
    )
    projected = lax.all_to_all(columns, ("dev", "role"), split_axis=0, concat_axis=1, tiled=True)
    widened = residual.astype(jnp.float32) + projected
    widened = widened.astype(jnp.bfloat16).astype(jnp.float32)
    normed = (
        widened * lax.rsqrt(jnp.mean(widened * widened, axis=-1, keepdims=True) + 1e-06) * norm_gain
    ).astype(jnp.bfloat16)
    flat_ids = expert_ids.reshape(count * TOP)
    expert_hits = (flat_ids[:, None] == jnp.arange(EXPERTS, dtype=jnp.int32)[None, :]).astype(
        jnp.int32
    )
    slot_index = jnp.sum((jnp.cumsum(expert_hits, axis=0) - 1) * expert_hits, axis=-1)
    position = flat_ids * capacity + slot_index
    placement = (
        position[:, None] == jnp.arange(EXPERTS * capacity, dtype=jnp.int32)[None, :]
    ).astype(jnp.float32)
    placement = placement.reshape(count, TOP, EXPERTS * capacity)
    assign = jnp.sum(placement, axis=1).astype(jnp.bfloat16)
    send_buffer = jnp.einsum(
        "rs,rd->sd", assign, normed, preferred_element_type=jnp.float32
    ).astype(jnp.bfloat16)
    combine_weights = jnp.einsum("rk,rks->rs", gate_weights, placement)
    slots_here = w_gate.shape[0]
    devices = lax.axis_size(("dev", "role"))
    doubled = jnp.broadcast_to(
        send_buffer.reshape(EXPERTS, 1, capacity, width), (EXPERTS, 2, capacity, width)
    )
    outgoing = doubled.reshape(devices, slots_here, capacity, width)
    produced = expert_work(
        lax.all_to_all(outgoing, ("dev", "role"), split_axis=0, concat_axis=0, tiled=True),
        w_gate,
        w_up,
        w_down,
    )
    returned = lax.all_to_all(
        produced.astype(jnp.bfloat16), ("dev", "role"), split_axis=0, concat_axis=0, tiled=True
    ).astype(produced.dtype)
    expert_out = jnp.sum(returned.reshape(EXPERTS, 2, capacity, width), axis=1)
    routed = jnp.dot(
        combine_weights,
        expert_out.reshape(EXPERTS * capacity, width),
        precision=lax.Precision.HIGHEST,
    )
    return (widened + routed).astype(jnp.bfloat16)


GATE_SLOTS = 5
DOWN_SLOTS = 3
MESH = pl.DeviceIdType.MESH


def layer_kernel(
    roles,
    att_ref,
    small_ref,
    proj_ref,
    gain_ref,
    wg_ref,
    wu_ref,
    wd_ref,
    out_ref,
    att_all,
    small_all,
    hid_all,
    normed,
    activation,
    total,
    part,
    got_core,
    got_row,
    got_col,
    gate_up,
    down,
    gate_sem,
    down_sem,
    att_send,
    att_recv,
    small_send,
    small_recv,
    hid_send,
    hid_recv,
    core_send,
    core_recv,
    row_send,
    row_recv,
    col_send,
    col_recv,
):
    devs = 4
    devices = devs * roles
    grp = lax.axis_index("grp")
    dev = lax.axis_index("dev")
    role = lax.axis_index("role")
    me = dev * roles + role
    sibling = dev + 1 - 2 * lax.rem(dev, 2)
    across = lax.rem(dev + 2, 4)
    diagonal = lax.rem(sibling + 2, 4)
    slots, width, half = wg_ref.shape
    pairs = slots // 2
    columns = proj_ref.shape[1]
    rows = 8
    tokens = devices * rows
    folded = width // 2

    def gate_copies(s, slot):
        return (
            pltpu.make_async_copy(
                wg_ref.at[s], gate_up.at[slot, :, pl.ds(0, half)], gate_sem.at[slot, 0]
            ),
            pltpu.make_async_copy(
                wu_ref.at[s], gate_up.at[slot, :, pl.ds(half, half)], gate_sem.at[slot, 1]
            ),
        )

    def down_copy(e, slot):
        return pltpu.make_async_copy(
            wd_ref.at[pl.ds(2 * e, 2)], down.at[slot], down_sem.at[slot]
        )

    for s in range(min(GATE_SLOTS, slots)):
        for copy in gate_copies(s, s):
            copy.start()
        if s % 2 == 1 and s // 2 < min(DOWN_SLOTS, pairs):
            down_copy(s // 2, s // 2).start()
    for e in range(min(GATE_SLOTS, slots) // 2, min(DOWN_SLOTS, pairs)):
        down_copy(e, e).start()

    def coords(k):
        other = lax.rem(me + k, devices)
        return other, (grp, other // roles, lax.rem(other, roles))

    barrier = pltpu.get_barrier_semaphore()
    for k in range(1, devices):
        pl.semaphore_signal(barrier, inc=1, device_id=coords(k)[1], device_id_type=MESH)
    pl.semaphore_wait(barrier, devices - 1)

    def send(src, dst, send_sem, recv_sem, target):
        copy = pltpu.make_async_remote_copy(
            src_ref=src,
            dst_ref=dst,
            send_sem=send_sem,
            recv_sem=recv_sem,
            device_id=target,
            device_id_type=MESH,
        )
        copy.start()
        return copy

    def gather(buf, send_sem, recv_sem, used):
        started = []

        def push(rank, target):
            started.append(
                send(
                    buf.at[rank],
                    buf.at[rank],
                    send_sem.at[len(started)],
                    recv_sem.at[rank],
                    target,
                )
            )

        def arrived(rank):
            pltpu.make_async_copy(buf.at[rank], buf.at[rank], recv_sem.at[rank]).wait()

        for k in range(1, roles):
            push(me, (grp, dev, lax.rem(role + k, roles)))
        push(me, (grp, across, role))
        push(me, (grp, sibling, role))
        used(me)
        for k in range(1, roles):
            rank = dev * roles + lax.rem(role + roles - k, roles)
            arrived(rank)
            push(rank, (grp, across, role))
            push(rank, (grp, sibling, role))
            used(rank)
        for k in range(roles):
            rank = across * roles + lax.rem(role + roles - k, roles)
            arrived(rank)
            push(rank, (grp, sibling, role))
            used(rank)
        for owner in (sibling, diagonal):
            for k in range(roles):
                rank = owner * roles + lax.rem(role + roles - k, roles)
                arrived(rank)
                used(rank)
        return started

    att_all[me] = att_ref[...]
    small_all[me] = small_ref[me]
    small_copies = []
    for k in range(1, devices):
        other, target = coords(k)
        small_copies.append(
            send(
                small_ref.at[other],
                small_all.at[me],
                small_send.at[k],
                small_recv.at[k],
                target,
            )
        )
    started = gather(att_all, att_send, att_recv, lambda rank: None)
    for copy in small_copies:
        copy.wait_recv()

    left = att_all[...].reshape(devices * 16, folded)
    low = jnp.dot(left, proj_ref[:folded, :], preferred_element_type=jnp.float32)
    high = jnp.dot(left, proj_ref[folded:, :], preferred_element_type=jnp.float32)
    low = low.reshape(devices, 16, columns)[:, :rows]
    high = high.reshape(devices, 16, columns)[:, rows:]
    hidden = small_all[:, :, :columns] + (low + high)
    hid_all[me] = hidden.reshape(tokens, columns).astype(jnp.bfloat16)
    weights = small_all[:, :, columns:].reshape(tokens, 128)
    lane = lax.broadcasted_iota(jnp.int32, (tokens, 128), 1)

    squares = [jnp.zeros((tokens, columns), jnp.float32)]

    def add_squares(rank):
        block = hid_all[rank].astype(jnp.float32)
        squares[0] = squares[0] + block * block

    started += gather(hid_all, hid_send, hid_recv, add_squares)
    mean = jnp.sum(squares[0], axis=1, keepdims=True) / width
    scale = lax.rsqrt(mean + 1e-06)

    for k in range(devices):
        cols = slice(k * columns, (k + 1) * columns)
        block = hid_all[k].astype(jnp.float32)
        normed[:, cols] = (block * scale * gain_ref[:, cols]).astype(jnp.bfloat16)

    def one_pair(e, carry):
        expert = me * pairs + e
        weight = jnp.sum(jnp.where(lane == expert, weights, 0.0), axis=1, keepdims=True)

        def one_half(j, inner):
            s = 2 * e + j
            slot = lax.rem(s, GATE_SLOTS)
            for copy in gate_copies(s, slot):
                copy.wait()
            both = jnp.dot(normed[...], gate_up[slot], preferred_element_type=jnp.float32)
            gate = both[:, :half]
            value = gate / (1.0 + jnp.exp(-gate)) * both[:, half:] * weight
            activation[j] = value.astype(jnp.bfloat16)

            @pl.when(s + GATE_SLOTS < slots)
            def _():
                for copy in gate_copies(s + GATE_SLOTS, slot):
                    copy.start()

            return inner

        lax.fori_loop(0, 2, one_half, 0)
        slot = lax.rem(e, DOWN_SLOTS)
        down_copy(e, slot).wait()
        act = jnp.concatenate([activation[0], activation[1]], axis=1)

        def one_chunk(c, inner):
            cols = pl.ds(pl.multiple_of(c * 512, 512), 512)
            piece = jnp.dot(
                act,
                down[slot, :, :, cols].reshape(2 * half, 512),
                preferred_element_type=jnp.float32,
            )

            @pl.when(e == 0)
            def _():
                total[:, cols] = piece

            @pl.when(e > 0)
            def _():
                total[:, cols] = total[:, cols] + piece

            return inner

        lax.fori_loop(0, width // 512, one_chunk, 0)

        @pl.when(e + DOWN_SLOTS < pairs)
        def _():
            down_copy(e + DOWN_SLOTS, slot).start()

        return carry

    lax.fori_loop(0, pairs, one_pair, 0)

    for c in range(folded // 256):
        lower = total[:, c * 256 : (c + 1) * 256].reshape(devs, roles, rows, 256)
        upper = total[:, folded + c * 256 : folded + (c + 1) * 256].reshape(
            devs, roles, rows, 256
        )
        part[:, :, :, c * 256 : (c + 1) * 256] = jnp.concatenate(
            [lower, upper], axis=2
        ).astype(jnp.bfloat16)

    first = send(
        part.at[diagonal], got_core.at[1], core_send.at[1], core_recv.at[1], (grp, sibling, role)
    )
    second = send(
        part.at[sibling], got_core.at[0], core_send.at[0], core_recv.at[0], (grp, sibling, role)
    )
    started += [first, second]
    first.wait_recv()
    part[across] = (
        part[across].astype(jnp.float32) + got_core[1].astype(jnp.float32)
    ).astype(jnp.bfloat16)
    crossing = send(
        part.at[across], got_row, row_send.at[0], row_recv.at[0], (grp, across, role)
    )
    started.append(crossing)
    second.wait_recv()
    crossing.wait_recv()
    part[dev] = (
        part[dev].astype(jnp.float32)
        + got_core[0].astype(jnp.float32)
        + got_row[...].astype(jnp.float32)
    ).astype(jnp.bfloat16)
    along = []
    for k in range(1, roles):
        other = lax.rem(role + k, roles)
        along.append(
            send(
                part.at[dev, other],
                got_col.at[k - 1],
                col_send.at[k - 1],
                col_recv.at[k - 1],
                (grp, dev, other),
            )
        )
    started += along

    mine = (
        lax.broadcasted_iota(jnp.int32, (rows, tokens), 1)
        == lax.broadcasted_iota(jnp.int32, (rows, tokens), 0) + me * rows
    ).astype(jnp.bfloat16)
    own = [
        jnp.dot(mine, hid_all[k], preferred_element_type=jnp.float32) for k in range(devices)
    ]
    for copy in along:
        copy.wait_recv()
    routed = part[dev, role].astype(jnp.float32)
    for k in range(roles - 1):
        routed = routed + got_col[k].astype(jnp.float32)
    for k in range(devices):
        at = k * columns
        piece = routed[:rows, at : at + columns] if at < folded else (
            routed[rows:, at - folded : at - folded + columns]
        )
        out_ref[:, at : at + columns] = (own[k] + piece).astype(jnp.bfloat16)
    for copy in started:
        copy.wait_send()
    for copy in small_copies:
        copy.wait_send()


def fused_body(
    roles,
    queries,
    key_cache,
    value_cache,
    new_key,
    new_value,
    lengths,
    residual,
    out_proj,
    norm_gain,
    expert_ids,
    gate_weights,
    w_gate,
    w_up,
    w_down,
):
    devices = 4 * roles
    count, width = residual.shape
    columns = out_proj.shape[1]
    half = w_gate.shape[2]
    attended = attend_rows(queries, key_cache, value_cache, new_key, new_value, lengths)
    attended = attended.reshape(count, 2, width // 2).swapaxes(0, 1).reshape(16, width // 2)
    named = expert_ids[:, :, None] == jnp.arange(128, dtype=jnp.int32)[None, None, :]
    combine = jnp.sum(jnp.where(named, gate_weights[:, :, None], 0.0), axis=1)
    small = jnp.concatenate(
        [
            residual.astype(jnp.float32).reshape(count, devices, columns).swapaxes(0, 1),
            jnp.broadcast_to(combine[None], (devices, count, 128)),
        ],
        axis=2,
    )
    tokens = devices * count
    dma = pltpu.SemaphoreType.DMA
    vmem = pl.BlockSpec(memory_space=pltpu.VMEM)
    hbm = pl.BlockSpec(memory_space=pl.ANY)
    bf16 = jnp.bfloat16
    return pl.pallas_call(
        functools.partial(layer_kernel, roles),
        out_shape=jax.ShapeDtypeStruct((count, width), bf16),
        in_specs=[vmem] * 4 + [hbm] * 3,
        out_specs=vmem,
        scratch_shapes=[
            pltpu.VMEM((devices, 16, width // 2), bf16),
            pltpu.VMEM((devices, count, columns + 128), jnp.float32),
            pltpu.VMEM((devices, tokens, columns), bf16),
            pltpu.VMEM((tokens, width), bf16),
            pltpu.VMEM((2, tokens, half), bf16),
            pltpu.VMEM((tokens, width), jnp.float32),
            pltpu.VMEM((4, roles, 16, width // 2), bf16),
            pltpu.VMEM((2, roles, 16, width // 2), bf16),
            pltpu.VMEM((roles, 16, width // 2), bf16),
            pltpu.VMEM((roles - 1, 16, width // 2), bf16),
            pltpu.VMEM((GATE_SLOTS, width, 2 * half), bf16),
            pltpu.VMEM((DOWN_SLOTS, 2, half, width), bf16),
            dma((GATE_SLOTS, 2)),
            dma((DOWN_SLOTS,)),
            dma((devices - 1,)),
            dma((devices,)),
            dma((devices,)),
            dma((devices,)),
            dma((devices - 1,)),
            dma((devices,)),
            dma((2,)),
            dma((2,)),
            dma((1,)),
            dma((1,)),
            dma((roles - 1,)),
            dma((roles - 1,)),
        ],
        compiler_params=pltpu.CompilerParams(
            collective_id=0, has_side_effects=True, vmem_limit_bytes=62 * 1024 * 1024
        ),
    )(attended, small, out_proj, norm_gain.reshape(1, width), w_gate, w_up, w_down)


def solution(mesh):
    placed = (
        P(("grp", "dev", "role"), None),
        P(("grp", "dev", "role"), None, None),
        P(("grp", "dev", "role"), None, None),
        P(("grp", "dev", "role"), None),
        P(("grp", "dev", "role"), None),
        P(("grp", "dev", "role")),
        P(("grp", "dev", "role"), None),
        P(None, ("dev", "role")),
        P(),
        P(("grp", "dev", "role"), None),
        P(("grp", "dev", "role"), None),
        P(("dev", "role"), None, None),
        P(("dev", "role"), None, None),
        P(("dev", "role"), None, None),
    )
    devs, roles = mesh.shape["dev"], mesh.shape["role"]
    fits = devs == 4 and roles == 4
    chosen = functools.partial(fused_body, roles) if fits else body
    return jax.shard_map(
        chosen, mesh=mesh, in_specs=placed, out_specs=P(("grp", "dev", "role"), None), check_vma=False
    )
```

```python
import functools

import jax
import jax.numpy as jnp
from jax import lax
from jax.experimental import pallas as pl
from jax.experimental.pallas import tpu as pltpu
from jax.sharding import PartitionSpec as P

QH = 32
KV = 4
HD = 128
EXPERTS = 64
TOP = 8
CTX = 128


def attend_rows(queries, key_cache, value_cache, new_key, new_value, lengths):
    count = queries.shape[0]
    grouped = queries.reshape(count, KV, QH // KV, HD)
    cached_keys = key_cache.reshape(count, CTX, KV, HD)
    cached_values = value_cache.reshape(count, CTX, KV, HD)
    fresh_key = new_key.reshape(count, KV, HD)
    fresh_value = new_value.reshape(count, KV, HD).astype(jnp.float32)
    scaling = HD ** (-0.5)
    scores = (
        jnp.einsum("rkgd,rtkd->rkgt", grouped, cached_keys, preferred_element_type=jnp.float32)
        * scaling
    )
    own_score = (
        jnp.einsum("rkgd,rkd->rkg", grouped, fresh_key, preferred_element_type=jnp.float32)
        * scaling
    )
    visible = jnp.arange(CTX, dtype=jnp.int32)[None, :] < lengths[:, None]
    scores = jnp.where(visible[:, None, None, :], scores, -jnp.inf)
    highest = jnp.maximum(jnp.max(scores, axis=-1), own_score)
    weights = jnp.exp(scores - highest[..., None])
    own_weight = jnp.exp(own_score - highest)
    total = jnp.sum(weights, axis=-1) + own_weight
    probs = (weights / total[..., None]).astype(jnp.bfloat16)
    own_prob = (own_weight / total).astype(jnp.bfloat16)
    combined = jnp.einsum(
        "rkgt,rtkd->rkgd", probs, cached_values, preferred_element_type=jnp.float32
    )
    combined = combined + own_prob.astype(jnp.float32)[..., None] * fresh_value[:, :, None, :]
    return combined.reshape(count, QH * HD).astype(jnp.bfloat16)


def expert_work(inputs, w_gate, w_up, w_down):
    gate_value = jnp.einsum("pscd,sdh->psch", inputs, w_gate, preferred_element_type=jnp.float32)
    up_value = jnp.einsum("pscd,sdh->psch", inputs, w_up, preferred_element_type=jnp.float32)
    activation = (jax.nn.silu(gate_value) * up_value).astype(jnp.bfloat16)
    return jnp.einsum("psch,shd->pscd", activation, w_down, preferred_element_type=jnp.float32)


def body(
    queries,
    key_cache,
    value_cache,
    new_key,
    new_value,
    lengths,
    residual,
    out_proj,
    norm_gain,
    expert_ids,
    gate_weights,
    w_gate,
    w_up,
    w_down,
):
    count = queries.shape[0]
    capacity = count // 4
    width = residual.shape[1]
    attended = attend_rows(queries, key_cache, value_cache, new_key, new_value, lengths)
    columns = jnp.dot(
        lax.all_gather(attended, ("dev", "role"), axis=0, tiled=True),
        out_proj,
        preferred_element_type=jnp.float32,
    )
    projected = lax.all_to_all(columns, ("dev", "role"), split_axis=0, concat_axis=1, tiled=True)
    widened = residual.astype(jnp.float32) + projected
    widened = widened.astype(jnp.bfloat16).astype(jnp.float32)
    normed = (
        widened * lax.rsqrt(jnp.mean(widened * widened, axis=-1, keepdims=True) + 1e-06) * norm_gain
    ).astype(jnp.bfloat16)
    flat_ids = expert_ids.reshape(count * TOP)
    expert_hits = (flat_ids[:, None] == jnp.arange(EXPERTS, dtype=jnp.int32)[None, :]).astype(
        jnp.int32
    )
    slot_index = jnp.sum((jnp.cumsum(expert_hits, axis=0) - 1) * expert_hits, axis=-1)
    position = flat_ids * capacity + slot_index
    placement = (
        position[:, None] == jnp.arange(EXPERTS * capacity, dtype=jnp.int32)[None, :]
    ).astype(jnp.float32)
    placement = placement.reshape(count, TOP, EXPERTS * capacity)
    assign = jnp.sum(placement, axis=1).astype(jnp.bfloat16)
    send_buffer = jnp.einsum(
        "rs,rd->sd", assign, normed, preferred_element_type=jnp.float32
    ).astype(jnp.bfloat16)
    combine_weights = jnp.einsum("rk,rks->rs", gate_weights, placement)
    slots_here = w_gate.shape[0]
    devices = lax.axis_size(("dev", "role"))
    doubled = jnp.broadcast_to(
        send_buffer.reshape(EXPERTS, 1, capacity, width), (EXPERTS, 2, capacity, width)
    )
    outgoing = doubled.reshape(devices, slots_here, capacity, width)
    produced = expert_work(
        lax.all_to_all(outgoing, ("dev", "role"), split_axis=0, concat_axis=0, tiled=True),
        w_gate,
        w_up,
        w_down,
    )
    returned = lax.all_to_all(
        produced.astype(jnp.bfloat16), ("dev", "role"), split_axis=0, concat_axis=0, tiled=True
    ).astype(produced.dtype)
    expert_out = jnp.sum(returned.reshape(EXPERTS, 2, capacity, width), axis=1)
    routed = jnp.dot(
        combine_weights,
        expert_out.reshape(EXPERTS * capacity, width),
        precision=lax.Precision.HIGHEST,
    )
    return (widened + routed).astype(jnp.bfloat16)


GATE_SLOTS = 5
DOWN_SLOTS = 3
CHUNKS = 4
MESH = pl.DeviceIdType.MESH


def layer_kernel(
    roles,
    att_ref,
    residual_ref,
    ids_ref,
    mix_ref,
    proj_ref,
    gain_ref,
    wg_ref,
    wu_ref,
    wd_ref,
    out_ref,
    att_all,
    small_out,
    small_all,
    own,
    hid_all,
    normed,
    activation,
    part,
    got_core,
    got_row,
    got_col,
    gate_up,
    down,
    gate_sem,
    down_sem,
    att_send,
    att_recv,
    small_send,
    small_recv,
    hid_send,
    hid_recv,
    core_send,
    core_recv,
    row_send,
    row_recv,
    col_send,
    col_recv,
):
    devs = 4
    devices = devs * roles
    grp = lax.axis_index("grp")
    dev = lax.axis_index("dev")
    role = lax.axis_index("role")
    me = dev * roles + role
    sibling = dev + 1 - 2 * lax.rem(dev, 2)
    across = lax.rem(dev + 2, 4)
    diagonal = lax.rem(sibling + 2, 4)
    slots, width, half = wg_ref.shape
    pairs = slots // 2
    columns = proj_ref.shape[1]
    rows = 8
    tokens = devices * rows
    folded = width // 2
    span = folded // CHUNKS

    def gate_copies(s, slot):
        return (
            pltpu.make_async_copy(
                wg_ref.at[s], gate_up.at[slot, :, pl.ds(0, half)], gate_sem.at[slot, 0]
            ),
            pltpu.make_async_copy(
                wu_ref.at[s], gate_up.at[slot, :, pl.ds(half, half)], gate_sem.at[slot, 1]
            ),
        )

    def down_copies(c):
        slot = c % DOWN_SLOTS
        return [
            pltpu.make_async_copy(
                wd_ref.at[:, :, pl.ds(j * folded + c * span, span)],
                down.at[slot, j],
                down_sem.at[slot, j],
            )
            for j in range(2)
        ]

    for s in range(min(GATE_SLOTS, slots)):
        for copy in gate_copies(s, s):
            copy.start()
    for c in range(DOWN_SLOTS):
        for copy in down_copies(c):
            copy.start()

    def coords(k):
        other = lax.rem(me + k, devices)
        return other, (grp, other // roles, lax.rem(other, roles))

    barrier = pltpu.get_barrier_semaphore()
    for k in range(1, devices):
        pl.semaphore_signal(barrier, inc=1, device_id=coords(k)[1], device_id_type=MESH)

    combine = jnp.zeros((rows, 128), jnp.float32)
    column = lax.broadcasted_iota(jnp.int32, (rows, 128), 1)
    for k in range(TOP):
        combine += jnp.where(column == ids_ref[:, k : k + 1], mix_ref[:, k : k + 1], 0.0)
    for k in range(devices):
        small_out[k, :, :columns] = residual_ref[:, k * columns : (k + 1) * columns].astype(
            jnp.float32
        )
        small_out[k, :, columns:] = combine
    att_all[me] = att_ref[...]
    small_all[me] = small_out[me]
    pl.semaphore_wait(barrier, devices - 1)

    def send(src, dst, send_sem, recv_sem, target):
        copy = pltpu.make_async_remote_copy(
            src_ref=src,
            dst_ref=dst,
            send_sem=send_sem,
            recv_sem=recv_sem,
            device_id=target,
            device_id_type=MESH,
        )
        copy.start()
        return copy

    def gather(buf, send_sem, recv_sem, used):
        started = []

        def push(rank, target):
            started.append(
                send(
                    buf.at[rank],
                    buf.at[rank],
                    send_sem.at[len(started)],
                    recv_sem.at[rank],
                    target,
                )
            )

        def arrived(rank):
            pltpu.make_async_copy(buf.at[rank], buf.at[rank], recv_sem.at[rank]).wait()

        for k in range(1, roles):
            push(me, (grp, dev, lax.rem(role + k, roles)))
        push(me, (grp, across, role))
        push(me, (grp, sibling, role))
        used(me)
        for k in range(1, roles):
            rank = dev * roles + lax.rem(role + roles - k, roles)
            arrived(rank)
            push(rank, (grp, across, role))
            push(rank, (grp, sibling, role))
            used(rank)
        for k in range(roles):
            rank = across * roles + lax.rem(role + roles - k, roles)
            arrived(rank)
            push(rank, (grp, sibling, role))
            used(rank)
        for owner in (sibling, diagonal):
            for k in range(roles):
                rank = owner * roles + lax.rem(role + roles - k, roles)
                arrived(rank)
                used(rank)
        return started

    small_copies = []
    for k in range(1, devices):
        other, target = coords(k)
        small_copies.append(
            send(
                small_out.at[other],
                small_all.at[me],
                small_send.at[k],
                small_recv.at[k],
                target,
            )
        )
    started = gather(att_all, att_send, att_recv, lambda rank: None)
    for copy in small_copies:
        copy.wait_recv()

    left = att_all[...].reshape(devices * 16, folded)
    low = jnp.dot(left, proj_ref[:folded, :], preferred_element_type=jnp.float32)
    high = jnp.dot(left, proj_ref[folded:, :], preferred_element_type=jnp.float32)
    low = low.reshape(devices, 16, columns)[:, :rows]
    high = high.reshape(devices, 16, columns)[:, rows:]
    hidden = small_all[:, :, :columns] + (low + high)
    hid_all[me] = hidden.reshape(tokens, columns).astype(jnp.bfloat16)
    weights = small_all[:, :, columns:].reshape(tokens, 128)
    lane = lax.broadcasted_iota(jnp.int32, (tokens, 128), 1)

    squares = [jnp.zeros((tokens, columns), jnp.float32)]

    def add_squares(rank):
        block = hid_all[rank].astype(jnp.float32)
        squares[0] = squares[0] + block * block

    started += gather(hid_all, hid_send, hid_recv, add_squares)
    mean = jnp.sum(squares[0], axis=1, keepdims=True) / width
    scale = lax.rsqrt(mean + 1e-06)

    for k in range(devices):
        cols = slice(k * columns, (k + 1) * columns)
        block = hid_all[k].astype(jnp.float32)
        normed[:, cols] = (block * scale * gain_ref[:, cols]).astype(jnp.bfloat16)

    def one_half(s, carry):
        expert = me * pairs + s // 2
        weight = jnp.sum(jnp.where(lane == expert, weights, 0.0), axis=1, keepdims=True)
        slot = lax.rem(s, GATE_SLOTS)
        for copy in gate_copies(s, slot):
            copy.wait()
        both = jnp.dot(normed[...], gate_up[slot], preferred_element_type=jnp.float32)
        gate = both[:, :half]
        value = gate / (1.0 + jnp.exp(-gate)) * both[:, half:] * weight
        activation[:, pl.ds(pl.multiple_of(s * half, 128), half)] = value.astype(jnp.bfloat16)

        @pl.when(s + GATE_SLOTS < slots)
        def _():
            for copy in gate_copies(s + GATE_SLOTS, slot):
                copy.start()

        return carry

    lax.fori_loop(0, slots, one_half, 0)

    to_core, to_row, to_col = {}, {}, {}

    def share(c):
        slot = c % DOWN_SLOTS
        for copy in down_copies(c):
            copy.wait()
        lower, upper = [
            jnp.dot(
                activation[...],
                down[slot, j].reshape(slots * half, span),
                preferred_element_type=jnp.float32,
            ).reshape(devs, roles, rows, span)
            for j in range(2)
        ]
        if c + DOWN_SLOTS < CHUNKS:
            for copy in down_copies(c + DOWN_SLOTS):
                copy.start()
        part[c] = jnp.concatenate([lower, upper], axis=2).astype(jnp.bfloat16)
        to_core[c] = [
            send(
                part.at[c, owner],
                got_core.at[c, j],
                core_send.at[c, j],
                core_recv.at[c, j],
                (grp, sibling, role),
            )
            for j, owner in ((1, diagonal), (0, sibling))
        ]

    def cross(c):
        to_core[c][0].wait_recv()
        part[c, across] = (
            part[c, across].astype(jnp.float32) + got_core[c, 1].astype(jnp.float32)
        ).astype(jnp.bfloat16)
        to_row[c] = send(
            part.at[c, across],
            got_row.at[c],
            row_send.at[c],
            row_recv.at[c],
            (grp, across, role),
        )

    def finish(c):
        to_core[c][1].wait_recv()
        to_row[c].wait_recv()
        part[c, dev] = (
            part[c, dev].astype(jnp.float32)
            + got_core[c, 0].astype(jnp.float32)
            + got_row[c].astype(jnp.float32)
        ).astype(jnp.bfloat16)
        to_col[c] = []
        for k in range(1, roles):
            other = lax.rem(role + k, roles)
            to_col[c].append(
                send(
                    part.at[c, dev, other],
                    got_col.at[c, k - 1],
                    col_send.at[c, k - 1],
                    col_recv.at[c, k - 1],
                    (grp, dev, other),
                )
            )

    for c in range(CHUNKS):
        share(c)
        if c >= 1:
            cross(c - 1)
        if c >= 2:
            finish(c - 2)
    cross(CHUNKS - 1)
    finish(CHUNKS - 2)

    mine = (
        lax.broadcasted_iota(jnp.int32, (rows, tokens), 1)
        == lax.broadcasted_iota(jnp.int32, (rows, tokens), 0) + me * rows
    ).astype(jnp.bfloat16)
    for k in range(devices):
        own[:, k * columns : (k + 1) * columns] = jnp.dot(
            mine, hid_all[k], preferred_element_type=jnp.float32
        )
    finish(CHUNKS - 1)
    for c in range(CHUNKS):
        for copy in to_col[c]:
            copy.wait_recv()
        routed = part[c, dev, role].astype(jnp.float32)
        for k in range(roles - 1):
            routed = routed + got_col[c, k].astype(jnp.float32)
        for j in range(2):
            cols = slice(j * folded + c * span, j * folded + (c + 1) * span)
            out_ref[:, cols] = (own[:, cols] + routed[j * rows : (j + 1) * rows]).astype(
                jnp.bfloat16
            )
        started += to_core[c] + [to_row[c]] + to_col[c]
    for copy in started:
        copy.wait_send()
    for copy in small_copies:
        copy.wait_send()


def fused_body(
    roles,
    queries,
    key_cache,
    value_cache,
    new_key,
    new_value,
    lengths,
    residual,
    out_proj,
    norm_gain,
    expert_ids,
    gate_weights,
    w_gate,
    w_up,
    w_down,
):
    devices = 4 * roles
    count, width = residual.shape
    columns = out_proj.shape[1]
    slots, half = w_gate.shape[0], w_gate.shape[2]
    span = width // 2 // CHUNKS
    attended = attend_rows(queries, key_cache, value_cache, new_key, new_value, lengths)
    attended = attended.reshape(count, 2, width // 2).swapaxes(0, 1).reshape(16, width // 2)
    tokens = devices * count
    dma = pltpu.SemaphoreType.DMA
    vmem = pl.BlockSpec(memory_space=pltpu.VMEM)
    hbm = pl.BlockSpec(memory_space=pl.ANY)
    bf16 = jnp.bfloat16
    return pl.pallas_call(
        functools.partial(layer_kernel, roles),
        out_shape=jax.ShapeDtypeStruct((count, width), bf16),
        in_specs=[vmem] * 6 + [hbm] * 3,
        out_specs=vmem,
        scratch_shapes=[
            pltpu.VMEM((devices, 16, width // 2), bf16),
            pltpu.VMEM((devices, count, columns + 128), jnp.float32),
            pltpu.VMEM((devices, count, columns + 128), jnp.float32),
            pltpu.VMEM((count, width), jnp.float32),
            pltpu.VMEM((devices, tokens, columns), bf16),
            pltpu.VMEM((tokens, width), bf16),
            pltpu.VMEM((tokens, slots * half), bf16),
            pltpu.VMEM((CHUNKS, 4, roles, 16, span), bf16),
            pltpu.VMEM((CHUNKS, 2, roles, 16, span), bf16),
            pltpu.VMEM((CHUNKS, roles, 16, span), bf16),
            pltpu.VMEM((CHUNKS, roles - 1, 16, span), bf16),
            pltpu.VMEM((GATE_SLOTS, width, 2 * half), bf16),
            pltpu.VMEM((DOWN_SLOTS, 2, slots, half, span), bf16),
            dma((GATE_SLOTS, 2)),
            dma((DOWN_SLOTS, 2)),
            dma((devices - 1,)),
            dma((devices,)),
            dma((devices,)),
            dma((devices,)),
            dma((devices - 1,)),
            dma((devices,)),
            dma((CHUNKS, 2)),
            dma((CHUNKS, 2)),
            dma((CHUNKS,)),
            dma((CHUNKS,)),
            dma((CHUNKS, roles - 1)),
            dma((CHUNKS, roles - 1)),
        ],
        compiler_params=pltpu.CompilerParams(
            collective_id=0, has_side_effects=True, vmem_limit_bytes=62 * 1024 * 1024
        ),
    )(
        attended,
        residual,
        expert_ids,
        gate_weights,
        out_proj,
        norm_gain.reshape(1, width),
        w_gate,
        w_up,
        w_down,
    )


def solution(mesh):
    placed = (
        P(("grp", "dev", "role"), None),
        P(("grp", "dev", "role"), None, None),
        P(("grp", "dev", "role"), None, None),
        P(("grp", "dev", "role"), None),
        P(("grp", "dev", "role"), None),
        P(("grp", "dev", "role")),
        P(("grp", "dev", "role"), None),
        P(None, ("dev", "role")),
        P(),
        P(("grp", "dev", "role"), None),
        P(("grp", "dev", "role"), None),
        P(("dev", "role"), None, None),
        P(("dev", "role"), None, None),
        P(("dev", "role"), None, None),
    )
    devs, roles = mesh.shape["dev"], mesh.shape["role"]
    fits = devs == 4 and roles == 4
    chosen = functools.partial(fused_body, roles) if fits else body
    return jax.shard_map(
        chosen, mesh=mesh, in_specs=placed, out_specs=P(("grp", "dev", "role"), None), check_vma=False
    )
```

```python
import functools

import jax
import jax.numpy as jnp
from jax import lax
from jax.experimental import pallas as pl
from jax.experimental.pallas import tpu as pltpu
from jax.sharding import PartitionSpec as P

QH = 32
KV = 4
HD = 128
EXPERTS = 64
TOP = 8
CTX = 128


def attend_rows(queries, key_cache, value_cache, new_key, new_value, lengths):
    count = queries.shape[0]
    grouped = queries.reshape(count, KV, QH // KV, HD)
    cached_keys = key_cache.reshape(count, CTX, KV, HD)
    cached_values = value_cache.reshape(count, CTX, KV, HD)
    fresh_key = new_key.reshape(count, KV, HD)
    fresh_value = new_value.reshape(count, KV, HD).astype(jnp.float32)
    scaling = HD ** (-0.5)
    scores = (
        jnp.einsum("rkgd,rtkd->rkgt", grouped, cached_keys, preferred_element_type=jnp.float32)
        * scaling
    )
    own_score = (
        jnp.einsum("rkgd,rkd->rkg", grouped, fresh_key, preferred_element_type=jnp.float32)
        * scaling
    )
    visible = jnp.arange(CTX, dtype=jnp.int32)[None, :] < lengths[:, None]
    scores = jnp.where(visible[:, None, None, :], scores, -jnp.inf)
    highest = jnp.maximum(jnp.max(scores, axis=-1), own_score)
    weights = jnp.exp(scores - highest[..., None])
    own_weight = jnp.exp(own_score - highest)
    total = jnp.sum(weights, axis=-1) + own_weight
    probs = (weights / total[..., None]).astype(jnp.bfloat16)
    own_prob = (own_weight / total).astype(jnp.bfloat16)
    combined = jnp.einsum(
        "rkgt,rtkd->rkgd", probs, cached_values, preferred_element_type=jnp.float32
    )
    combined = combined + own_prob.astype(jnp.float32)[..., None] * fresh_value[:, :, None, :]
    return combined.reshape(count, QH * HD).astype(jnp.bfloat16)


def expert_work(inputs, w_gate, w_up, w_down):
    gate_value = jnp.einsum("pscd,sdh->psch", inputs, w_gate, preferred_element_type=jnp.float32)
    up_value = jnp.einsum("pscd,sdh->psch", inputs, w_up, preferred_element_type=jnp.float32)
    activation = (jax.nn.silu(gate_value) * up_value).astype(jnp.bfloat16)
    return jnp.einsum("psch,shd->pscd", activation, w_down, preferred_element_type=jnp.float32)


def body(
    queries,
    key_cache,
    value_cache,
    new_key,
    new_value,
    lengths,
    residual,
    out_proj,
    norm_gain,
    expert_ids,
    gate_weights,
    w_gate,
    w_up,
    w_down,
):
    count = queries.shape[0]
    capacity = count // 4
    width = residual.shape[1]
    attended = attend_rows(queries, key_cache, value_cache, new_key, new_value, lengths)
    columns = jnp.dot(
        lax.all_gather(attended, ("dev", "role"), axis=0, tiled=True),
        out_proj,
        preferred_element_type=jnp.float32,
    )
    projected = lax.all_to_all(columns, ("dev", "role"), split_axis=0, concat_axis=1, tiled=True)
    widened = residual.astype(jnp.float32) + projected
    widened = widened.astype(jnp.bfloat16).astype(jnp.float32)
    normed = (
        widened * lax.rsqrt(jnp.mean(widened * widened, axis=-1, keepdims=True) + 1e-06) * norm_gain
    ).astype(jnp.bfloat16)
    flat_ids = expert_ids.reshape(count * TOP)
    expert_hits = (flat_ids[:, None] == jnp.arange(EXPERTS, dtype=jnp.int32)[None, :]).astype(
        jnp.int32
    )
    slot_index = jnp.sum((jnp.cumsum(expert_hits, axis=0) - 1) * expert_hits, axis=-1)
    position = flat_ids * capacity + slot_index
    placement = (
        position[:, None] == jnp.arange(EXPERTS * capacity, dtype=jnp.int32)[None, :]
    ).astype(jnp.float32)
    placement = placement.reshape(count, TOP, EXPERTS * capacity)
    assign = jnp.sum(placement, axis=1).astype(jnp.bfloat16)
    send_buffer = jnp.einsum(
        "rs,rd->sd", assign, normed, preferred_element_type=jnp.float32
    ).astype(jnp.bfloat16)
    combine_weights = jnp.einsum("rk,rks->rs", gate_weights, placement)
    slots_here = w_gate.shape[0]
    devices = lax.axis_size(("dev", "role"))
    doubled = jnp.broadcast_to(
        send_buffer.reshape(EXPERTS, 1, capacity, width), (EXPERTS, 2, capacity, width)
    )
    outgoing = doubled.reshape(devices, slots_here, capacity, width)
    produced = expert_work(
        lax.all_to_all(outgoing, ("dev", "role"), split_axis=0, concat_axis=0, tiled=True),
        w_gate,
        w_up,
        w_down,
    )
    returned = lax.all_to_all(
        produced.astype(jnp.bfloat16), ("dev", "role"), split_axis=0, concat_axis=0, tiled=True
    ).astype(produced.dtype)
    expert_out = jnp.sum(returned.reshape(EXPERTS, 2, capacity, width), axis=1)
    routed = jnp.dot(
        combine_weights,
        expert_out.reshape(EXPERTS * capacity, width),
        precision=lax.Precision.HIGHEST,
    )
    return (widened + routed).astype(jnp.bfloat16)


GATE_SLOTS = 5
DOWN_SLOTS = 3
CHUNKS = 4
MESH = pl.DeviceIdType.MESH


def layer_kernel(
    roles,
    att_ref,
    residual_ref,
    ids_ref,
    mix_ref,
    proj_ref,
    gain_ref,
    wg_ref,
    wu_ref,
    wd_ref,
    out_ref,
    att_all,
    small_out,
    small_all,
    own,
    hid_all,
    normed,
    activation,
    part,
    early,
    got_core,
    got_row,
    got_col,
    gate_up,
    down,
    gate_sem,
    down_sem,
    att_send,
    att_recv,
    small_send,
    small_recv,
    hid_send,
    hid_recv,
    core_send,
    core_recv,
    row_send,
    row_recv,
    col_send,
    col_recv,
):
    devs = 4
    devices = devs * roles
    grp = lax.axis_index("grp")
    dev = lax.axis_index("dev")
    role = lax.axis_index("role")
    me = dev * roles + role
    sibling = dev + 1 - 2 * lax.rem(dev, 2)
    across = lax.rem(dev + 2, 4)
    diagonal = lax.rem(sibling + 2, 4)
    slots, width, half = wg_ref.shape
    pairs = slots // 2
    columns = proj_ref.shape[1]
    rows = 8
    tokens = devices * rows
    folded = width // 2
    span = folded // CHUNKS

    def gate_copies(s, slot):
        return (
            pltpu.make_async_copy(
                wg_ref.at[s], gate_up.at[slot, :, pl.ds(0, half)], gate_sem.at[slot, 0]
            ),
            pltpu.make_async_copy(
                wu_ref.at[s], gate_up.at[slot, :, pl.ds(half, half)], gate_sem.at[slot, 1]
            ),
        )

    def down_copies(c):
        slot = c % DOWN_SLOTS
        return [
            pltpu.make_async_copy(
                wd_ref.at[:, :, pl.ds(j * folded + c * span, span)],
                down.at[slot, j],
                down_sem.at[slot, j],
            )
            for j in range(2)
        ]

    for s in range(min(GATE_SLOTS, slots)):
        for copy in gate_copies(s, s):
            copy.start()
    for c in range(DOWN_SLOTS):
        for copy in down_copies(c):
            copy.start()

    def coords(k):
        other = lax.rem(me + k, devices)
        return other, (grp, other // roles, lax.rem(other, roles))

    barrier = pltpu.get_barrier_semaphore()
    for k in range(1, devices):
        pl.semaphore_signal(barrier, inc=1, device_id=coords(k)[1], device_id_type=MESH)

    combine = jnp.zeros((rows, 128), jnp.float32)
    column = lax.broadcasted_iota(jnp.int32, (rows, 128), 1)
    for k in range(TOP):
        combine += jnp.where(column == ids_ref[:, k : k + 1], mix_ref[:, k : k + 1], 0.0)
    for k in range(devices):
        small_out[k, :, :columns] = residual_ref[:, k * columns : (k + 1) * columns].astype(
            jnp.float32
        )
        small_out[k, :, columns:] = combine
    att_all[me] = att_ref[...]
    small_all[me] = small_out[me]
    pl.semaphore_wait(barrier, devices - 1)

    def send(src, dst, send_sem, recv_sem, target):
        copy = pltpu.make_async_remote_copy(
            src_ref=src,
            dst_ref=dst,
            send_sem=send_sem,
            recv_sem=recv_sem,
            device_id=target,
            device_id_type=MESH,
        )
        copy.start()
        return copy

    def gather(buf, send_sem, recv_sem, used):
        started = []

        def push(rank, target):
            started.append(
                send(
                    buf.at[rank],
                    buf.at[rank],
                    send_sem.at[len(started)],
                    recv_sem.at[rank],
                    target,
                )
            )

        def arrived(rank):
            pltpu.make_async_copy(buf.at[rank], buf.at[rank], recv_sem.at[rank]).wait()

        for k in range(1, roles):
            push(me, (grp, dev, lax.rem(role + k, roles)))
        push(me, (grp, across, role))
        push(me, (grp, sibling, role))
        used(me)
        for k in range(1, roles):
            rank = dev * roles + lax.rem(role + roles - k, roles)
            arrived(rank)
            push(rank, (grp, across, role))
            push(rank, (grp, sibling, role))
            used(rank)
        for k in range(roles):
            rank = across * roles + lax.rem(role + roles - k, roles)
            arrived(rank)
            push(rank, (grp, sibling, role))
            used(rank)
        for owner in (sibling, diagonal):
            for k in range(roles):
                rank = owner * roles + lax.rem(role + roles - k, roles)
                arrived(rank)
                used(rank)
        return started

    small_copies = []
    for k in range(1, devices):
        other, target = coords(k)
        small_copies.append(
            send(
                small_out.at[other],
                small_all.at[me],
                small_send.at[k],
                small_recv.at[k],
                target,
            )
        )
    started = gather(att_all, att_send, att_recv, lambda rank: None)
    for copy in small_copies:
        copy.wait_recv()

    left = att_all[...].reshape(devices * 16, folded)
    low = jnp.dot(left, proj_ref[:folded, :], preferred_element_type=jnp.float32)
    high = jnp.dot(left, proj_ref[folded:, :], preferred_element_type=jnp.float32)
    low = low.reshape(devices, 16, columns)[:, :rows]
    high = high.reshape(devices, 16, columns)[:, rows:]
    hidden = small_all[:, :, :columns] + (low + high)
    hid_all[me] = hidden.reshape(tokens, columns).astype(jnp.bfloat16)
    weights = small_all[:, :, columns:].reshape(tokens, 128)
    lane = lax.broadcasted_iota(jnp.int32, (tokens, 128), 1)

    squares = [jnp.zeros((tokens, columns), jnp.float32)]
    seen = []
    ready = min(GATE_SLOTS, slots)
    group = roles * columns

    def use(rank):
        block = hid_all[rank].astype(jnp.float32)
        squares[0] = squares[0] + block * block
        cols = pl.ds(pl.multiple_of(rank * columns, columns), columns)
        normed[:, cols] = (block * gain_ref[:, cols]).astype(jnp.bfloat16)
        seen.append(rank)
        if len(seen) % roles:
            return
        owner = (dev, across, sibling, diagonal)[len(seen) // roles - 1]
        part_of = pl.ds(pl.multiple_of(owner * group, group), group)
        opening = len(seen) == roles

        def one_slot(slot, carry):
            if opening:
                for copy in gate_copies(slot, slot):
                    copy.wait()
            piece = jnp.dot(
                normed[:, part_of],
                gate_up[slot, part_of, :],
                preferred_element_type=jnp.float32,
            )
            early[slot] = piece if opening else early[slot] + piece
            return carry

        lax.fori_loop(0, ready, one_slot, 0)

    started += gather(hid_all, hid_send, hid_recv, use)
    for s in range(ready, slots):
        for copy in gate_copies(s, s - ready):
            copy.start()
    mean = jnp.sum(squares[0], axis=1, keepdims=True) / width
    scale = lax.rsqrt(mean + 1e-06)

    def activate(s, both):
        expert = me * pairs + s // 2
        weight = jnp.sum(jnp.where(lane == expert, weights, 0.0), axis=1, keepdims=True)
        gate = both[:, :half] * scale
        value = gate / (1.0 + jnp.exp(-gate)) * (both[:, half:] * scale) * weight
        activation[:, pl.ds(pl.multiple_of(s * half, 128), half)] = value.astype(jnp.bfloat16)

    def from_early(s, carry):
        activate(s, early[s])
        return carry

    lax.fori_loop(0, ready, from_early, 0)

    def from_late(s, carry):
        slot = s - ready
        for copy in gate_copies(s, slot):
            copy.wait()
        activate(
            s, jnp.dot(normed[...], gate_up[slot], preferred_element_type=jnp.float32)
        )
        return carry

    lax.fori_loop(ready, slots, from_late, 0)

    to_core, to_row, to_col = {}, {}, {}

    def share(c):
        slot = c % DOWN_SLOTS
        for copy in down_copies(c):
            copy.wait()
        lower, upper = [
            jnp.dot(
                activation[...],
                down[slot, j].reshape(slots * half, span),
                preferred_element_type=jnp.float32,
            ).reshape(devs, roles, rows, span)
            for j in range(2)
        ]
        if c + DOWN_SLOTS < CHUNKS:
            for copy in down_copies(c + DOWN_SLOTS):
                copy.start()
        part[c] = jnp.concatenate([lower, upper], axis=2).astype(jnp.bfloat16)
        to_core[c] = [
            send(
                part.at[c, owner],
                got_core.at[c, j],
                core_send.at[c, j],
                core_recv.at[c, j],
                (grp, sibling, role),
            )
            for j, owner in ((1, diagonal), (0, sibling))
        ]

    def cross(c):
        to_core[c][0].wait_recv()
        part[c, across] = (
            part[c, across].astype(jnp.float32) + got_core[c, 1].astype(jnp.float32)
        ).astype(jnp.bfloat16)
        to_row[c] = send(
            part.at[c, across],
            got_row.at[c],
            row_send.at[c],
            row_recv.at[c],
            (grp, across, role),
        )

    def finish(c):
        to_core[c][1].wait_recv()
        to_row[c].wait_recv()
        part[c, dev] = (
            part[c, dev].astype(jnp.float32)
            + got_core[c, 0].astype(jnp.float32)
            + got_row[c].astype(jnp.float32)
        ).astype(jnp.bfloat16)
        to_col[c] = []
        for k in range(1, roles):
            other = lax.rem(role + k, roles)
            to_col[c].append(
                send(
                    part.at[c, dev, other],
                    got_col.at[c, k - 1],
                    col_send.at[c, k - 1],
                    col_recv.at[c, k - 1],
                    (grp, dev, other),
                )
            )

    for c in range(CHUNKS):
        share(c)
        if c >= 1:
            cross(c - 1)
        if c >= 2:
            finish(c - 2)
    cross(CHUNKS - 1)
    finish(CHUNKS - 2)

    mine = (
        lax.broadcasted_iota(jnp.int32, (rows, tokens), 1)
        == lax.broadcasted_iota(jnp.int32, (rows, tokens), 0) + me * rows
    ).astype(jnp.bfloat16)
    for k in range(devices):
        own[:, k * columns : (k + 1) * columns] = jnp.dot(
            mine, hid_all[k], preferred_element_type=jnp.float32
        )
    finish(CHUNKS - 1)
    for c in range(CHUNKS):
        for copy in to_col[c]:
            copy.wait_recv()
        routed = part[c, dev, role].astype(jnp.float32)
        for k in range(roles - 1):
            routed = routed + got_col[c, k].astype(jnp.float32)
        for j in range(2):
            cols = slice(j * folded + c * span, j * folded + (c + 1) * span)
            out_ref[:, cols] = (own[:, cols] + routed[j * rows : (j + 1) * rows]).astype(
                jnp.bfloat16
            )
        started += to_core[c] + [to_row[c]] + to_col[c]
    for copy in started:
        copy.wait_send()
    for copy in small_copies:
        copy.wait_send()


def fused_body(
    roles,
    queries,
    key_cache,
    value_cache,
    new_key,
    new_value,
    lengths,
    residual,
    out_proj,
    norm_gain,
    expert_ids,
    gate_weights,
    w_gate,
    w_up,
    w_down,
):
    devices = 4 * roles
    count, width = residual.shape
    columns = out_proj.shape[1]
    slots, half = w_gate.shape[0], w_gate.shape[2]
    span = width // 2 // CHUNKS
    attended = attend_rows(queries, key_cache, value_cache, new_key, new_value, lengths)
    attended = attended.reshape(count, 2, width // 2).swapaxes(0, 1).reshape(16, width // 2)
    tokens = devices * count
    dma = pltpu.SemaphoreType.DMA
    vmem = pl.BlockSpec(memory_space=pltpu.VMEM)
    hbm = pl.BlockSpec(memory_space=pl.ANY)
    bf16 = jnp.bfloat16
    return pl.pallas_call(
        functools.partial(layer_kernel, roles),
        out_shape=jax.ShapeDtypeStruct((count, width), bf16),
        in_specs=[vmem] * 6 + [hbm] * 3,
        out_specs=vmem,
        scratch_shapes=[
            pltpu.VMEM((devices, 16, width // 2), bf16),
            pltpu.VMEM((devices, count, columns + 128), jnp.float32),
            pltpu.VMEM((devices, count, columns + 128), jnp.float32),
            pltpu.VMEM((count, width), jnp.float32),
            pltpu.VMEM((devices, tokens, columns), bf16),
            pltpu.VMEM((tokens, width), bf16),
            pltpu.VMEM((tokens, slots * half), bf16),
            pltpu.VMEM((CHUNKS, 4, roles, 16, span), bf16),
            pltpu.VMEM((min(GATE_SLOTS, slots), tokens, 2 * half), jnp.float32),
            pltpu.VMEM((CHUNKS, 2, roles, 16, span), bf16),
            pltpu.VMEM((CHUNKS, roles, 16, span), bf16),
            pltpu.VMEM((CHUNKS, roles - 1, 16, span), bf16),
            pltpu.VMEM((GATE_SLOTS, width, 2 * half), bf16),
            pltpu.VMEM((DOWN_SLOTS, 2, slots, half, span), bf16),
            dma((GATE_SLOTS, 2)),
            dma((DOWN_SLOTS, 2)),
            dma((devices - 1,)),
            dma((devices,)),
            dma((devices,)),
            dma((devices,)),
            dma((devices - 1,)),
            dma((devices,)),
            dma((CHUNKS, 2)),
            dma((CHUNKS, 2)),
            dma((CHUNKS,)),
            dma((CHUNKS,)),
            dma((CHUNKS, roles - 1)),
            dma((CHUNKS, roles - 1)),
        ],
        compiler_params=pltpu.CompilerParams(
            collective_id=0, has_side_effects=True, vmem_limit_bytes=62 * 1024 * 1024
        ),
    )(
        attended,
        residual,
        expert_ids,
        gate_weights,
        out_proj,
        norm_gain.reshape(1, width),
        w_gate,
        w_up,
        w_down,
    )


def solution(mesh):
    placed = (
        P(("grp", "dev", "role"), None),
        P(("grp", "dev", "role"), None, None),
        P(("grp", "dev", "role"), None, None),
        P(("grp", "dev", "role"), None),
        P(("grp", "dev", "role"), None),
        P(("grp", "dev", "role")),
        P(("grp", "dev", "role"), None),
        P(None, ("dev", "role")),
        P(),
        P(("grp", "dev", "role"), None),
        P(("grp", "dev", "role"), None),
        P(("dev", "role"), None, None),
        P(("dev", "role"), None, None),
        P(("dev", "role"), None, None),
    )
    devs, roles = mesh.shape["dev"], mesh.shape["role"]
    fits = devs == 4 and roles == 4
    chosen = functools.partial(fused_body, roles) if fits else body
    return jax.shard_map(
        chosen, mesh=mesh, in_specs=placed, out_specs=P(("grp", "dev", "role"), None), check_vma=False
    )
```
